32 devices in a mesh: dp: 8 (over z, x), width: 2 (over y), grid: 2 (over core).
Axes of the slice: x: 2, y: 2, z: 4, core: 2. Of those that a mesh axis runs over, the one named last changes fastest.
Arguments:
- train_acts: bfloat16 [6144, 16384], P(('dp', 'grid'), 'width'), may hold values from -6 to 6
- train_grads: bfloat16 [6144, 16384], P(('dp', 'grid'), 'width'), may hold values from -6 to 6
- query_acts: bfloat16 [512, 16384], P('dp', 'width'), may hold values from -6 to 6
- query_grads: bfloat16 [512, 16384], P('dp', 'width'), may hold values from -6 to 6
- act_inverse: bfloat16 [16384, 16384], P(('dp', 'grid'), 'width'), may hold values from -0.046875 to 0.046875
- grad_inverse: bfloat16 [16384, 16384], P(('dp', 'grid'), 'width'), may hold values from -0.046875 to 0.046875
- query_slot: int32 [16], replicated, may hold values from 0 to 15, each once
- resident: int32 [6144], P(('dp', 'grid')), may hold values 0 or 1
Outputs:
- scores: float32 [6144, 16], P(('dp', 'grid'), 'width')
The draws below stay inside these ranges and needn't reach their ends.
All inputs are finite; a program needn't handle non-finite values. No bound on the sum of `resident` on one device may be relied on, other than what follows from the above.
Results may differ from the reference program's by a relative error of at most 0.0041.
Values may be sent and summed in bfloat16 or wider, within the bound.
A program may use at most 128 MiB of HBM per device.

```python
import math
import jax
import jax.numpy as jnp
from jax import lax

D = 16384
QDIM = 16384
QUERIES = 16
QTOK = 32
QROWS = 512
TRAIN = 6144


def with_ends(values, stream_key, smallest, high):
    longest = values.shape.index(max(values.shape))
    spots = []
    for shift in (0, 1):
        where = [jax.random.randint(jax.random.fold_in(stream_key, axis), (), 0, length) for axis, length in enumerate(values.shape)]
        where[longest] = (where[longest] + shift) % values.shape[longest]
        spots.append(tuple(where))
    return values.at[spots[0]].set(smallest).at[spots[1]].set(high)


def levels(stream_key, shape, cuts, least, high):
    def one(dim, shards_of):
        draws = jax.random.uniform(jax.random.fold_in(jax.random.fold_in(stream_key, 6), dim), (shards_of,), jnp.float32, least / len(cuts), high / len(cuts))
        return jnp.repeat(jnp.exp(draws), shape[dim] // shards_of).reshape((-1,) + (1,) * (len(shape) - dim - 1))

    loudness = one(*cuts[0])
    for cut in cuts[1:]:
        loudness = loudness * one(*cut)
    return loudness


def noise(rng, dims, spread, limit, split=(), kind=jnp.bfloat16):
    result = jax.random.normal(rng, dims, jnp.float32) * spread
    if len(split) > 0:
        result = levels(rng, dims, split, -0.22, 0.18) * result
    return jnp.clip(result, min=-limit, max=limit).astype(kind)


def setup_inputs(seed: int = 0) -> dict:
    splits = jax.random.split(jax.random.key(seed), 9)
    train_acts = noise(splits[0], (TRAIN, D), 1.0, 6.0, ((0, 16), (1, 2)))
    train_grads = noise(splits[1], (TRAIN, QDIM), 1.0, 6.0, ((0, 16), (1, 2)))
    query_acts = noise(splits[2], (QROWS, D), 1.0, 6.0, ((0, 8), (1, 2)))
    query_grads = noise(splits[3], (QROWS, QDIM), 1.0, 6.0, ((0, 8), (1, 2)))
    act_inverse = noise(splits[4], (D, D), D ** -0.5, 0.046875, ((0, 16), (1, 2)))
    grad_inverse = noise(splits[5], (QDIM, QDIM), QDIM ** -0.5, 0.046875, ((0, 16), (1, 2)))
    query_slot = jax.random.permutation(splits[6], QUERIES).astype(jnp.int32)
    resident = with_ends((jax.random.randint(splits[7], (TRAIN,), 0, 4) < 3).astype(jnp.int32), jax.random.fold_in(splits[7], 1), 0, 1)
    return {"train_acts": train_acts, "train_grads": train_grads, "query_acts": query_acts, "query_grads": query_grads, "act_inverse": act_inverse, "grad_inverse": grad_inverse, "query_slot": query_slot, "resident": resident}


def reference(train_acts, train_grads, query_acts, query_grads, act_inverse, grad_inverse, query_slot, resident):
    act_factor = jnp.dot(act_inverse, query_acts.T, preferred_element_type=jnp.float32).astype(jnp.bfloat16)
    grad_factor = jnp.dot(grad_inverse, query_grads.T, preferred_element_type=jnp.float32).astype(jnp.bfloat16)
    act_proj = jnp.dot(train_acts, act_factor, preferred_element_type=jnp.float32)
    grad_proj = jnp.dot(train_grads, grad_factor, preferred_element_type=jnp.float32)
    factor_scale = 1.0 / (D * math.sqrt(QTOK))
    influence = lax.optimization_barrier(jnp.sum((act_proj * grad_proj).reshape(act_proj.shape[0], QUERIES, QTOK), axis=2)) * factor_scale
    source = jnp.zeros((QUERIES,), jnp.int32).at[query_slot].set(jnp.arange(QUERIES, dtype=jnp.int32))
    return influence[:, source] * resident[:, None].astype(jnp.float32)
```

```python
import functools
import math

import jax
import jax.numpy as jnp
from jax import lax
from jax.experimental import pallas as pl
from jax.experimental.pallas import tpu as pltpu
from jax.sharding import PartitionSpec as P

LANES = 2
CUTS = 2
PARTS = 2
BLOCKS = 4
VMEM = 62 * 1024 * 1024


def pipeline(
    n_dp, n_width, n_grid, seg_sum,
    qa, qg, ia, ig, ta, tg, out,
    qbuf, ibuf, part, rs, mine, fac, proj, prs, infl,
    load_sem, inv_sem, train_sem,
    a_recv, a_core, a_send,
    rs_send, rs_recv, w_send, w_recv,
    c_recv, c_core, c_send,
    p_send, p_recv, f_send, f_recv,
):
    dp, w, g = lax.axis_index("dp"), lax.axis_index("width"), lax.axis_index("grid")
    line = n_dp // LANES
    z, x = dp // LANES, lax.rem(dp, LANES)
    q_hbm, inv_hbm, train_hbm = (qa, qg), (ia, ig), (ta, tg)
    q_rows = qa.shape[0]
    half = q_rows // n_grid
    feats = qa.shape[1] // CUTS
    rows = ia.shape[0]
    block = rows // BLOCKS
    cut = rows // PARTS
    tokens = ta.shape[0]
    cols = part.shape[-1]
    group = n_dp // n_width
    home = dp // group
    slot = lax.rem(dp, group)

    def device(d=None, width=None, grid=None):
        return {
            "dp": dp if d is None else d,
            "width": w if width is None else width,
            "grid": g if grid is None else grid,
        }

    def remote(src, dst, send, recv, to):
        return pltpu.make_async_remote_copy(
            src_ref=src, dst_ref=dst, send_sem=send, recv_sem=recv,
            device_id=to, device_id_type=pl.DeviceIdType.MESH,
        )

    def other(j):
        return lax.rem(w + j, n_width)

    class Gather:
        def __init__(self, ref, recv, core, send, lo, count, own_core):
            self.ref, self.recv, self.core, self.send = ref, recv, core, send
            self.lo, self.count, self.own_core = lo, count, own_core

        def copy(self, o, lane, d):
            ref = self.ref(o, lane, g)
            if d == 0:
                to = device((z + 1) * LANES + x)
            elif d == 1:
                to = device((z - 1) * LANES + x)
            elif d < 1 + LANES:
                to = device(z * LANES + lax.rem(x + d - 1, LANES))
            else:
                to = device(grid=lax.rem(g + d - LANES, n_grid))
            recv = self.recv(o, lane) if d < 1 + LANES else self.core(o, lane, g)
            return remote(ref, ref, self.send(o, lane, d), recv, to)

        def wait(self, o, lane):
            self.copy(o, lane, 2).wait_recv()

        def has(self, o):
            return (o >= self.lo) & (o < self.lo + self.count)

        def sends(self, o, lane, up, down, across, core, act):
            if up:
                pl.when(z + 1 < line)(lambda: act(self.copy(o, lane, 0)))
            if down:
                pl.when(z > 0)(lambda: act(self.copy(o, lane, 1)))
            if across:
                for d in range(2, 1 + LANES):
                    act(self.copy(o, lane, d))
            if core:
                for d in range(1 + LANES, LANES + n_grid):
                    act(self.copy(o, lane, d))

        def walk(self, act, stage, step):
            first = act is not None
            run = act if first else (lambda c: c.wait_send())
            if stage == 0:
                pl.when(self.has(z))(
                    lambda: self.sends(z, x, True, True, True, self.own_core, run))
            elif stage == 1:
                for o, up in ((z - step, True), (z + step, False)):
                    @pl.when(self.has(o))
                    def _(o=o, up=up):
                        if first:
                            self.wait(o, x)
                        self.sends(o, x, up, not up, True, True, run)
            else:
                for o in (z,) if step == 0 else (z - step, z + step):
                    @pl.when(self.has(o))
                    def _(o=o):
                        for d in range(1, LANES):
                            lane = lax.rem(x + d, LANES)
                            if first:
                                self.wait(o, lane)
                            self.sends(o, lane, False, False, False, True, run)

        def start(self):
            self.walk(lambda c: c.start(), 0, 0)

        def along(self, step):
            self.walk(lambda c: c.start(), 1, step)

        def across(self, step):
            self.walk(lambda c: c.start(), 2, step)

        def finish(self):
            for i in range(self.count):
                o = self.lo + i
                for lane in range(LANES):
                    def _(o=o, lane=lane):
                        for j in range(1, n_grid):
                            src = lax.rem(g + j, n_grid)
                            ref = self.ref(o, lane, src)
                            remote(ref, ref, self.send(o, lane, 0), self.core(o, lane, src),
                                   device(grid=src)).wait_recv()
                    if self.own_core:
                        _()
                    else:
                        pl.when((o != z) | (lane != x))(_)

        def drain(self):
            self.walk(None, 0, 0)
            for step in range(1, line):
                self.walk(None, 1, step)
            for step in range(line):
                self.walk(None, 2, step)

    def query_gather(k):
        a, f = divmod(k, CUTS)

        def ref(o, lane, gg):
            at = pl.multiple_of((o * LANES + lane) * q_rows + gg * half, half)
            return qbuf.at[a, f, pl.ds(at, half)]

        return Gather(
            ref,
            lambda o, l: a_recv.at[k, o * LANES + l],
            lambda o, l, gg: a_core.at[k, o * LANES + l, gg],
            lambda o, l, d: a_send.at[k, o * LANES + l, d],
            0, line, False)

    lines = group // LANES

    def factor_gather(a, h, j):
        c = other(j)

        def local(o, l):
            return (o - w * lines) * LANES + l

        def ref(o, lane, gg):
            return fac.at[a, c, local(o, lane), gg, pl.ds(h * cut, cut)]

        return Gather(
            ref,
            lambda o, l: c_recv.at[a, h, c, local(o, l)],
            lambda o, l, gg: c_core.at[a, h, c, local(o, l), gg],
            lambda o, l, d: c_send.at[a, h, c, local(o, l), d],
            w * lines, lines, True)

    units = 2 * CUTS * BLOCKS

    def inv_load(u):
        k, rb = divmod(u, BLOCKS)
        a, f = divmod(k, CUTS)
        s = u % ibuf.shape[0]
        return pltpu.make_async_copy(
            inv_hbm[a].at[pl.ds(rb * block, block), pl.ds(f * feats, feats)],
            ibuf.at[s], inv_sem.at[s])

    def rs_copy(a, rb, j):
        c = other(j)
        at = pl.ds(rb * block, block)
        return remote(part.at[a, c, at], rs.at[a, n_width - 1 - j, at],
                      rs_send.at[a, rb, j], rs_recv.at[a, rb, j], device(width=c))

    def multiply(u):
        k, rb = divmod(u, BLOCKS)
        a, f = divmod(k, CUTS)
        ahead = u + ibuf.shape[0] - 1
        if ahead < units:
            inv_load(ahead).start()
        inv_load(u).wait()
        at = pl.ds(rb * block, block)
        left = ibuf[u % ibuf.shape[0]]
        wide = max(cols, min(256, cols * n_width))
        per = wide // cols
        for n in range(cols * n_width // wide):
            prod = lax.dot_general(
                left, qbuf[a, f, n * wide:(n + 1) * wide], (((1,), (1,)), ((), ())),
                preferred_element_type=jnp.float32)
            for i in range(per):
                piece = prod[:, i * cols:(i + 1) * cols]
                if f == 0:
                    part[a, n * per + i, at] = piece
                else:
                    part[a, n * per + i, at] += piece
        if f == CUTS - 1:
            for j in range(1, n_width):
                rs_copy(a, rb, j).start()

    def hand_copy(a, h, src_w, j):
        at = pl.ds(h * cut, cut)
        return remote(mine.at[a, at], fac.at[a, src_w, slot, g, at],
                      w_send.at[a, h], w_recv.at[a, h, j], device(width=home))

    def total(a, h):
        per = BLOCKS // PARTS
        for rb in range(h * per, (h + 1) * per):
            at = pl.ds(rb * block, block)
            for j in range(1, n_width):
                rs_copy(a, rb, j).wait_recv()
            value = part[a, w, at]
            for j in range(1, n_width):
                value = value + rs[a, n_width - 1 - j, at]
            value = value.astype(jnp.bfloat16)

            @pl.when(w == home)
            def _():
                fac[a, w, slot, g, at] = value

            @pl.when(w != home)
            def _():
                mine[a, at] = value

        @pl.when(w != home)
        def _():
            hand_copy(a, h, w, lax.rem(home - w + n_width, n_width)).start()

    def handed(a, h, j):
        if j > 0:
            @pl.when(w == home)
            def _():
                hand_copy(a, h, other(j), n_width - j).wait_recv()

    def train_load(a, f):
        return pltpu.make_async_copy(
            train_hbm[a].at[:, pl.ds(f * feats, feats)],
            qbuf.at[a, f, pl.ds(0, tokens)], train_sem.at[a, f])

    def project(a, h, c):
        acc = None
        for b in range(group * n_grid):
            at = b * rows + h * cut
            f, col = divmod(at, feats)
            term = jnp.dot(
                qbuf[a, f, 0:tokens, col:col + cut],
                fac[a, c, b // n_grid, b % n_grid, pl.ds(h * cut, cut)],
                preferred_element_type=jnp.float32)
            acc = term if acc is None else acc + term
        if h == 0:
            proj[a, c] = acc
        else:
            proj[a, c] += acc

    def p_copy(a, j):
        c = other(j)
        return remote(proj.at[a, c], prs.at[a, n_width - 1 - j],
                      p_send.at[a, j], p_recv.at[a, j], device(width=c))

    def f_copy(j):
        return remote(infl.at[w], infl.at[w], f_send.at[j], f_recv.at[j],
                      device(width=other(j)))

    own = pl.ds(pl.multiple_of(dp * q_rows, q_rows), q_rows)
    loads = []
    for a in range(2):
        for f in range(CUTS):
            loads.append(pltpu.make_async_copy(
                q_hbm[a].at[:, pl.ds(f * feats, feats)], qbuf.at[a, f, own],
                load_sem.at[a, f]))
            loads[-1].start()
    for u in range(ibuf.shape[0] - 1):
        inv_load(u).start()

    barrier = pltpu.get_barrier_semaphore()

    def hello(to):
        pl.semaphore_signal(barrier, inc=1, device_id=to, device_id_type=pl.DeviceIdType.MESH)

    pl.when(z + 1 < line)(lambda: hello(device((z + 1) * LANES + x)))
    pl.when(z > 0)(lambda: hello(device((z - 1) * LANES + x)))
    for j in range(1, LANES):
        hello(device(z * LANES + lax.rem(x + j, LANES)))
    for j in range(1, n_grid):
        hello(device(grid=lax.rem(g + j, n_grid)))
    for j in range(1, n_width):
        hello(device(width=other(j)))
    ends = jnp.where(z + 1 < line, 1, 0) + jnp.where(z > 0, 1, 0)
    pl.semaphore_wait(barrier, ends + (LANES - 1 + n_grid - 1 + n_width - 1))

    for load in loads:
        load.wait()

    chunks = [query_gather(k) for k in range(2 * CUTS)]
    factors = [[[factor_gather(a, h, j) for j in range(n_width)] for h in range(PARTS)]
               for a in range(2)]

    def run(todo, count):
        for _ in range(min(count, len(todo))):
            todo.pop(0)()

    def begin(a, h):
        for j in range(n_width):
            handed(a, h, j)
            factors[a][h][j].start()

    chunks[0].start()
    for k in range(2 * CUTS):
        chunk = chunks[k]
        todo = []
        if k > 0:
            todo = [functools.partial(multiply, (k - 1) * BLOCKS + b) for b in range(BLOCKS)]
        for step in range(1, line):
            chunk.along(step)
            run(todo, 1)
            if step == line - 1 and k + 1 < 2 * CUTS:
                chunks[k + 1].start()
            chunk.across(step - 1)
        run(todo, len(todo))
        if k == 2 * CUTS - 1:
            for h in range(PARTS):
                total(0, h)
            for h in range(PARTS):
                begin(0, h)
        chunk.across(line - 1)
        chunk.finish()

    def spread(a, todo):
        for h in range(PARTS):
            for step in range(1, line):
                for one in factors[a][h]:
                    one.along(step)
                run(todo, 1)
                for one in factors[a][h]:
                    one.across(step - 1)
            for one in factors[a][h]:
                one.across(line - 1)

    for f in range(CUTS):
        chunks[f].drain()
        train_load(0, f).start()
    todo = [functools.partial(multiply, (2 * CUTS - 1) * BLOCKS + b) for b in range(BLOCKS)]

    def second():
        for f in range(CUTS):
            chunks[CUTS + f].drain()
            train_load(1, f).start()

    todo.append(second)
    spread(0, todo)
    run(todo, len(todo))
    for h in range(PARTS):
        total(1, h)
    for h in range(PARTS):
        begin(1, h)
    for f in range(CUTS):
        train_load(0, f).wait()

    def first_proj(h):
        for one in factors[0][h]:
            one.finish()
        for c in range(n_width):
            project(0, h, c)

    def first_sends():
        for j in range(1, n_width):
            p_copy(0, j).start()

    todo = [functools.partial(first_proj, h) for h in range(PARTS)] + [first_sends]
    spread(1, todo)
    run(todo, len(todo))
    for f in range(CUTS):
        train_load(1, f).wait()
    for h in range(PARTS):
        for one in factors[1][h]:
            one.finish()
        for c in range(n_width):
            project(1, h, c)
    for j in range(1, n_width):
        p_copy(1, j).start()
    shares = []
    for a in range(2):
        for j in range(1, n_width):
            p_copy(a, j).wait_recv()
        value = proj[a, w]
        for j in range(1, n_width):
            value = value + prs[a, n_width - 1 - j]
        shares.append(value)
    per_seq = seg_sum[1]
    shape = (infl.shape[1], cols)
    pick = (lax.broadcasted_iota(jnp.int32, shape, 1) // per_seq
            == lax.broadcasted_iota(jnp.int32, shape, 0)).astype(jnp.float32)
    infl[w] = lax.dot_general(
        pick, shares[0] * shares[1], (((1,), (1,)), ((), ())),
        precision=lax.Precision.HIGHEST, preferred_element_type=jnp.float32) * seg_sum[0]
    for j in range(1, n_width):
        f_copy(j).start()

    for j in range(1, n_width):
        src = other(j)
        remote(infl.at[src], infl.at[src], f_send.at[j], f_recv.at[n_width - j],
               device(width=src)).wait_recv()
    out[...] = infl[...]
    for a in range(2):
        for h in range(PARTS):
            for one in factors[a][h]:
                one.drain()
            pl.when(w != home)(lambda a=a, h=h: hand_copy(a, h, w, 0).wait_send())
        for rb in range(BLOCKS):
            for j in range(1, n_width):
                rs_copy(a, rb, j).wait_send()
        for j in range(1, n_width):
            p_copy(a, j).wait_send()
    for j in range(1, n_width):
        f_copy(j).wait_send()


def solution(mesh):
    n_dp, n_width, n_grid = (mesh.shape[n] for n in ("dp", "width", "grid"))

    def local(train_acts, train_grads, query_acts, query_grads, act_inverse, grad_inverse,
              query_slot, resident):
        queries = query_slot.shape[0]
        q_all = query_acts.shape[0] * n_dp
        per_seq = q_all // queries
        depth = query_acts.shape[1]
        feats = depth // CUTS
        rows = act_inverse.shape[0]
        tokens = train_acts.shape[0]
        cols = q_all // n_width
        group = n_dp // n_width
        scale = 1.0 / (depth * n_width * math.sqrt(per_seq))
        bf, f32 = jnp.bfloat16, jnp.float32
        dma = pltpu.SemaphoreType.DMA
        ways = LANES + n_grid
        hbm = pl.BlockSpec(memory_space=pl.ANY)
        flops = 4 * rows * depth * q_all + 4 * tokens * depth * q_all
        moved = 4 * (rows + tokens + q_all) * depth
        table = pl.pallas_call(
            functools.partial(pipeline, n_dp, n_width, n_grid, (scale, per_seq)),
            out_shape=jax.ShapeDtypeStruct((n_width, queries // n_width, tokens), f32),
            in_specs=[hbm] * 6,
            out_specs=pl.BlockSpec(memory_space=pltpu.VMEM),
            scratch_shapes=[
                pltpu.VMEM((2, CUTS, q_all, feats), bf),
                pltpu.VMEM((3, rows // BLOCKS, feats), bf),
                pltpu.VMEM((2, n_width, rows, cols), f32),
                pltpu.VMEM((2, n_width - 1, rows, cols), f32),
                pltpu.VMEM((2, rows, cols), bf),
                pltpu.VMEM((2, n_width, group, n_grid, rows, cols), bf),
                pltpu.VMEM((2, n_width, tokens, cols), f32),
                pltpu.VMEM((2, n_width - 1, tokens, cols), f32),
                pltpu.VMEM((n_width, queries // n_width, tokens), f32),
                dma((2, CUTS)), dma((3,)), dma((2, CUTS)),
                dma((2 * CUTS, n_dp)), dma((2 * CUTS, n_dp, n_grid)), dma((2 * CUTS, n_dp, ways)),
                dma((2, BLOCKS, n_width)), dma((2, BLOCKS, n_width)),
                dma((2, PARTS)), dma((2, PARTS, n_width)),
                dma((2, PARTS, n_width, group)), dma((2, PARTS, n_width, group, n_grid)),
                dma((2, PARTS, n_width, group, ways)),
                dma((2, n_width)), dma((2, n_width)), dma((n_width,)), dma((n_width,)),
            ],
            compiler_params=pltpu.CompilerParams(
                collective_id=0, has_side_effects=True, vmem_limit_bytes=VMEM),
            cost_estimate=pl.CostEstimate(flops=flops, bytes_accessed=moved, transcendentals=0),
        )(query_acts, query_grads, act_inverse, grad_inverse, train_acts, train_grads)
        share = queries // n_width
        slots = lax.axis_index("width") * share + jnp.arange(share, dtype=jnp.int32)
        hit = query_slot[:, None] == slots[None, :]
        picked = jnp.sum(
            jnp.where(hit[:, :, None], table.reshape(queries, 1, tokens), 0.0), axis=0)
        return picked.T * resident[:, None].astype(f32)

    return jax.shard_map(
        local,
        mesh=mesh,
        in_specs=(
            P(("dp", "grid"), "width"),
            P(("dp", "grid"), "width"),
            P("dp", "width"),
            P("dp", "width"),
            P(("dp", "grid"), "width"),
            P(("dp", "grid"), "width"),
            P(),
            P(("dp", "grid")),
        ),
        out_specs=P(("dp", "grid"), "width"),
        check_vma=False,
    )
```

```python
import functools
import math

import jax
import jax.numpy as jnp
from jax import lax
from jax.experimental import pallas as pl
from jax.experimental.pallas import tpu as pltpu
from jax.sharding import PartitionSpec as P

LANES = 2
CUTS = 2
PARTS = 2
BLOCKS = 4
VMEM = 62 * 1024 * 1024


def pipeline(
    n_dp, n_width, n_grid, seg_sum,
    qa, qg, ia, ig, ta, tg, out,
    qbuf, ibuf, part, rs, mine, fac, proj, prs, infl,
    load_sem, inv_sem, train_sem,
    a_recv, a_core, a_send,
    rs_send, rs_recv, w_send, w_recv,
    c_recv, c_core, c_send,
    p_send, p_recv, f_send, f_recv,
):
    dp, w, g = lax.axis_index("dp"), lax.axis_index("width"), lax.axis_index("grid")
    line = n_dp // LANES
    z, x = dp // LANES, lax.rem(dp, LANES)
    q_hbm, inv_hbm, train_hbm = (qa, qg), (ia, ig), (ta, tg)
    q_rows = qa.shape[0]
    half = q_rows // n_grid
    feats = qa.shape[1] // CUTS
    rows = ia.shape[0]
    block = rows // BLOCKS
    cut = rows // PARTS
    tokens = ta.shape[0]
    cols = part.shape[-1]
    group = n_dp // n_width
    home = dp // group
    slot = lax.rem(dp, group)

    def device(d=None, width=None, grid=None):
        return {
            "dp": dp if d is None else d,
            "width": w if width is None else width,
            "grid": g if grid is None else grid,
        }

    def remote(src, dst, send, recv, to):
        return pltpu.make_async_remote_copy(
            src_ref=src, dst_ref=dst, send_sem=send, recv_sem=recv,
            device_id=to, device_id_type=pl.DeviceIdType.MESH,
        )

    def other(j):
        return lax.rem(w + j, n_width)

    class Gather:
        def __init__(self, ref, recv, core, send, lo, count, own_core, along=-1):
            self.through = along
            self.ref, self.recv, self.core, self.send = ref, recv, core, send
            self.lo, self.count, self.own_core = lo, count, own_core

        def copy(self, o, lane, d):
            ref = self.ref(o, lane, g)
            if d == 0:
                to = device((z + 1) * LANES + x)
            elif d == 1:
                to = device((z - 1) * LANES + x)
            elif d < 1 + LANES:
                to = device(z * LANES + lax.rem(x + d - 1, LANES))
            else:
                to = device(grid=lax.rem(g + d - LANES, n_grid))
            recv = self.recv(o, lane) if d < 1 + LANES else self.core(o, lane, g)
            return remote(ref, ref, self.send(o, lane, d), recv, to)

        def wait(self, o, lane):
            self.copy(o, lane, 2).wait_recv()

        def has(self, o):
            return (o >= self.lo) & (o < self.lo + self.count)

        def sends(self, o, lane, up, down, across, core, act):
            if up:
                pl.when(z + 1 < line)(lambda: act(self.copy(o, lane, 0)))
            if down:
                pl.when(z > 0)(lambda: act(self.copy(o, lane, 1)))
            if across:
                for d in range(2, 1 + LANES):
                    act(self.copy(o, lane, d))
            if core:
                for d in range(1 + LANES, LANES + n_grid):
                    act(self.copy(o, lane, d))

        def walk(self, act, stage, step):
            first = act is not None
            run = act if first else (lambda c: c.wait_send())
            if stage == 0:
                pl.when(self.has(z))(
                    lambda: self.sends(z, x, True, True, True, self.own_core, run))
            elif stage == 1:
                for o, up in ((z - step, True), (z + step, False)):
                    @pl.when(self.has(o))
                    def _(o=o, up=up):
                        if first:
                            self.wait(o, x)
                        self.sends(o, x, up, not up, False, True, run)
                        pl.when(o != self.through)(
                            lambda: self.sends(o, x, False, False, True, False, run))
            else:
                ways = ((z, True, True),) if step == 0 else (
                    (z - step, True, False), (z + step, False, True))
                for o, up, down in ways:
                    @pl.when(self.has(o))
                    def _(o=o, up=up, down=down):
                        for d in range(1, LANES):
                            lane = lax.rem(x + d, LANES)
                            if first:
                                self.wait(o, lane)
                            self.sends(o, lane, False, False, False, True, run)
                            pl.when(o == self.through)(
                                lambda: self.sends(o, lane, up, down, False, False, run))

        def start(self):
            self.walk(lambda c: c.start(), 0, 0)

        def along(self, step):
            self.walk(lambda c: c.start(), 1, step)

        def across(self, step):
            self.walk(lambda c: c.start(), 2, step)

        def finish(self):
            for i in range(self.count):
                o = self.lo + i
                for lane in range(LANES):
                    def _(o=o, lane=lane):
                        for j in range(1, n_grid):
                            src = lax.rem(g + j, n_grid)
                            ref = self.ref(o, lane, src)
                            remote(ref, ref, self.send(o, lane, 0), self.core(o, lane, src),
                                   device(grid=src)).wait_recv()
                    if self.own_core:
                        _()
                    else:
                        pl.when((o != z) | (lane != x))(_)

        def drain(self):
            self.walk(None, 0, 0)
            for step in range(1, line):
                self.walk(None, 1, step)
            for step in range(line):
                self.walk(None, 2, step)

    def query_gather(k):
        a, f = divmod(k, CUTS)

        def ref(o, lane, gg):
            at = pl.multiple_of((o * LANES + lane) * q_rows + gg * half, half)
            return qbuf.at[a, f, pl.ds(at, half)]

        return Gather(
            ref,
            lambda o, l: a_recv.at[k, o * LANES + l],
            lambda o, l, gg: a_core.at[k, o * LANES + l, gg],
            lambda o, l, d: a_send.at[k, o * LANES + l, d],
            0, line, False, 0 if k % 2 == 0 else line - 1)

    lines = group // LANES

    def factor_gather(a, h, j):
        c = other(j)

        def local(o, l):
            return (o - w * lines) * LANES + l

        def ref(o, lane, gg):
            return fac.at[a, c, local(o, lane), gg, pl.ds(h * cut, cut)]

        return Gather(
            ref,
            lambda o, l: c_recv.at[a, h, c, local(o, l)],
            lambda o, l, gg: c_core.at[a, h, c, local(o, l), gg],
            lambda o, l, d: c_send.at[a, h, c, local(o, l), d],
            w * lines, lines, True)

    units = 2 * CUTS * BLOCKS

    def inv_load(u):
        k, rb = divmod(u, BLOCKS)
        a, f = divmod(k, CUTS)
        s = u % ibuf.shape[0]
        return pltpu.make_async_copy(
            inv_hbm[a].at[pl.ds(rb * block, block), pl.ds(f * feats, feats)],
            ibuf.at[s], inv_sem.at[s])

    def rs_copy(a, rb, j):
        c = other(j)
        at = pl.ds(rb * block, block)
        return remote(part.at[a, c, at], rs.at[a, n_width - 1 - j, at],
                      rs_send.at[a, rb, j], rs_recv.at[a, rb, j], device(width=c))

    def multiply(u):
        k, rb = divmod(u, BLOCKS)
        a, f = divmod(k, CUTS)
        ahead = u + ibuf.shape[0] - 1
        if ahead < units:
            inv_load(ahead).start()
        inv_load(u).wait()
        at = pl.ds(rb * block, block)
        left = ibuf[u % ibuf.shape[0]]
        wide = max(cols, min(256, cols * n_width))
        per = wide // cols
        for n in range(cols * n_width // wide):
            prod = lax.dot_general(
                left, qbuf[a, f, n * wide:(n + 1) * wide], (((1,), (1,)), ((), ())),
                preferred_element_type=jnp.float32)
            for i in range(per):
                piece = prod[:, i * cols:(i + 1) * cols]
                if f == 0:
                    part[a, n * per + i, at] = piece
                else:
                    part[a, n * per + i, at] += piece
        if f == CUTS - 1:
            for j in range(1, n_width):
                rs_copy(a, rb, j).start()

    def hand_copy(a, h, src_w, j):
        at = pl.ds(h * cut, cut)
        return remote(mine.at[a, at], fac.at[a, src_w, slot, g, at],
                      w_send.at[a, h], w_recv.at[a, h, j], device(width=home))

    def total(a, h):
        per = BLOCKS // PARTS
        for rb in range(h * per, (h + 1) * per):
            at = pl.ds(rb * block, block)
            for j in range(1, n_width):
                rs_copy(a, rb, j).wait_recv()
            value = part[a, w, at]
            for j in range(1, n_width):
                value = value + rs[a, n_width - 1 - j, at]
            value = value.astype(jnp.bfloat16)

            @pl.when(w == home)
            def _():
                fac[a, w, slot, g, at] = value

            @pl.when(w != home)
            def _():
                mine[a, at] = value

        @pl.when(w != home)
        def _():
            hand_copy(a, h, w, lax.rem(home - w + n_width, n_width)).start()

    def handed(a, h, j):
        if j > 0:
            @pl.when(w == home)
            def _():
                hand_copy(a, h, other(j), n_width - j).wait_recv()

    def train_load(a, f):
        return pltpu.make_async_copy(
            train_hbm[a].at[:, pl.ds(f * feats, feats)],
            qbuf.at[a, f, pl.ds(0, tokens)], train_sem.at[a, f])

    def project(a, h, c):
        acc = None
        for b in range(group * n_grid):
            at = b * rows + h * cut
            f, col = divmod(at, feats)
            term = jnp.dot(
                qbuf[a, f, 0:tokens, col:col + cut],
                fac[a, c, b // n_grid, b % n_grid, pl.ds(h * cut, cut)],
                preferred_element_type=jnp.float32)
            acc = term if acc is None else acc + term
        if h == 0:
            proj[a, c] = acc
        else:
            proj[a, c] += acc

    def p_copy(a, j):
        c = other(j)
        return remote(proj.at[a, c], prs.at[a, n_width - 1 - j],
                      p_send.at[a, j], p_recv.at[a, j], device(width=c))

    def f_copy(j):
        return remote(infl.at[w], infl.at[w], f_send.at[j], f_recv.at[j],
                      device(width=other(j)))

    own = pl.ds(pl.multiple_of(dp * q_rows, q_rows), q_rows)
    loads = []
    for a in range(2):
        for f in range(CUTS):
            loads.append(pltpu.make_async_copy(
                q_hbm[a].at[:, pl.ds(f * feats, feats)], qbuf.at[a, f, own],
                load_sem.at[a, f]))
            loads[-1].start()
    for u in range(ibuf.shape[0] - 1):
        inv_load(u).start()

    barrier = pltpu.get_barrier_semaphore()

    def hello(to):
        pl.semaphore_signal(barrier, inc=1, device_id=to, device_id_type=pl.DeviceIdType.MESH)

    pl.when(z + 1 < line)(lambda: hello(device((z + 1) * LANES + x)))
    pl.when(z > 0)(lambda: hello(device((z - 1) * LANES + x)))
    for j in range(1, LANES):
        hello(device(z * LANES + lax.rem(x + j, LANES)))
    for j in range(1, n_grid):
        hello(device(grid=lax.rem(g + j, n_grid)))
    for j in range(1, n_width):
        hello(device(width=other(j)))
    ends = jnp.where(z + 1 < line, 1, 0) + jnp.where(z > 0, 1, 0)
    pl.semaphore_wait(barrier, ends + (LANES - 1 + n_grid - 1 + n_width - 1))

    for load in loads:
        load.wait()

    chunks = [query_gather(k) for k in range(2 * CUTS)]
    factors = [[[factor_gather(a, h, j) for j in range(n_width)] for h in range(PARTS)]
               for a in range(2)]

    def run(todo, count):
        for _ in range(min(count, len(todo))):
            todo.pop(0)()

    def begin_own(a):
        for h in range(PARTS):
            factors[a][h][0].start()

    def begin_rest(a):
        for h in range(PARTS):
            for j in range(1, n_width):
                handed(a, h, j)
                factors[a][h][j].start()

    chunks[0].start()
    for k in range(2 * CUTS):
        chunk = chunks[k]
        last = k == 2 * CUTS - 1
        todo, sums = [], []
        if k > 0:
            todo = [functools.partial(multiply, (k - 1) * BLOCKS + b) for b in range(BLOCKS)]
        if last:
            sums = [functools.partial(total, 0, h) for h in range(PARTS)]
        for step in range(1, line):
            chunk.along(step)
            run(todo, 1)
            run(sums, 1)
            if step == line - 1:
                if last:
                    run(sums, len(sums))
                    begin_own(0)
                else:
                    chunks[k + 1].start()
            chunk.across(step - 1)
        run(todo, len(todo))
        if last:
            begin_rest(0)
        chunk.across(line - 1)
        chunk.finish()

    def spread(a, todo):
        for h in range(PARTS):
            for step in range(1, line):
                for one in factors[a][h]:
                    one.along(step)
                run(todo, 1)
                for one in factors[a][h]:
                    one.across(step - 1)
            for one in factors[a][h]:
                one.across(line - 1)

    todo = [functools.partial(multiply, (2 * CUTS - 1) * BLOCKS + b) for b in range(BLOCKS)]
    run(todo, 2)

    def reuse(a):
        for f in range(CUTS):
            chunks[a * CUTS + f].drain()
            train_load(a, f).start()

    reuse(0)
    todo.append(functools.partial(reuse, 1))
    todo += [functools.partial(total, 1, h) for h in range(PARTS)]
    todo += [functools.partial(begin_own, 1), functools.partial(begin_rest, 1)]
    spread(0, todo)
    run(todo, len(todo))
    for f in range(CUTS):
        train_load(0, f).wait()

    def first_proj(h):
        for one in factors[0][h]:
            one.finish()
        for c in range(n_width):
            project(0, h, c)

    def first_sends():
        for j in range(1, n_width):
            p_copy(0, j).start()

    todo = [functools.partial(first_proj, h) for h in range(PARTS)] + [first_sends]
    spread(1, todo)
    run(todo, len(todo))
    for f in range(CUTS):
        train_load(1, f).wait()
    for h in range(PARTS):
        for one in factors[1][h]:
            one.finish()
        for j in [*range(1, n_width), 0]:
            project(1, h, other(j))
            if h == PARTS - 1 and j > 0:
                p_copy(1, j).start()
    shares = []
    for a in range(2):
        for j in range(1, n_width):
            p_copy(a, j).wait_recv()
        value = proj[a, w]
        for j in range(1, n_width):
            value = value + prs[a, n_width - 1 - j]
        shares.append(value)
    per_seq = seg_sum[1]
    shape = (infl.shape[1], cols)
    pick = (lax.broadcasted_iota(jnp.int32, shape, 1) // per_seq
            == lax.broadcasted_iota(jnp.int32, shape, 0)).astype(jnp.float32)
    infl[w] = lax.dot_general(
        pick, shares[0] * shares[1], (((1,), (1,)), ((), ())),
        precision=lax.Precision.HIGHEST, preferred_element_type=jnp.float32) * seg_sum[0]
    for j in range(1, n_width):
        f_copy(j).start()

    for j in range(1, n_width):
        src = other(j)
        remote(infl.at[src], infl.at[src], f_send.at[j], f_recv.at[n_width - j],
               device(width=src)).wait_recv()
    out[...] = infl[...]
    for a in range(2):
        for h in range(PARTS):
            for one in factors[a][h]:
                one.drain()
            pl.when(w != home)(lambda a=a, h=h: hand_copy(a, h, w, 0).wait_send())
        for rb in range(BLOCKS):
            for j in range(1, n_width):
                rs_copy(a, rb, j).wait_send()
        for j in range(1, n_width):
            p_copy(a, j).wait_send()
    for j in range(1, n_width):
        f_copy(j).wait_send()


def solution(mesh):
    n_dp, n_width, n_grid = (mesh.shape[n] for n in ("dp", "width", "grid"))

    def local(train_acts, train_grads, query_acts, query_grads, act_inverse, grad_inverse,
              query_slot, resident):
        queries = query_slot.shape[0]
        q_all = query_acts.shape[0] * n_dp
        per_seq = q_all // queries
        depth = query_acts.shape[1]
        feats = depth // CUTS
        rows = act_inverse.shape[0]
        tokens = train_acts.shape[0]
        cols = q_all // n_width
        group = n_dp // n_width
        scale = 1.0 / (depth * n_width * math.sqrt(per_seq))
        bf, f32 = jnp.bfloat16, jnp.float32
        dma = pltpu.SemaphoreType.DMA
        ways = LANES + n_grid
        hbm = pl.BlockSpec(memory_space=pl.ANY)
        flops = 4 * rows * depth * q_all + 4 * tokens * depth * q_all
        moved = 4 * (rows + tokens + q_all) * depth
        table = pl.pallas_call(
            functools.partial(pipeline, n_dp, n_width, n_grid, (scale, per_seq)),
            out_shape=jax.ShapeDtypeStruct((n_width, queries // n_width, tokens), f32),
            in_specs=[hbm] * 6,
            out_specs=pl.BlockSpec(memory_space=pltpu.VMEM),
            scratch_shapes=[
                pltpu.VMEM((2, CUTS, q_all, feats), bf),
                pltpu.VMEM((3, rows // BLOCKS, feats), bf),
                pltpu.VMEM((2, n_width, rows, cols), f32),
                pltpu.VMEM((2, n_width - 1, rows, cols), f32),
                pltpu.VMEM((2, rows, cols), bf),
                pltpu.VMEM((2, n_width, group, n_grid, rows, cols), bf),
                pltpu.VMEM((2, n_width, tokens, cols), f32),
                pltpu.VMEM((2, n_width - 1, tokens, cols), f32),
                pltpu.VMEM((n_width, queries // n_width, tokens), f32),
                dma((2, CUTS)), dma((3,)), dma((2, CUTS)),
                dma((2 * CUTS, n_dp)), dma((2 * CUTS, n_dp, n_grid)), dma((2 * CUTS, n_dp, ways)),
                dma((2, BLOCKS, n_width)), dma((2, BLOCKS, n_width)),
                dma((2, PARTS)), dma((2, PARTS, n_width)),
                dma((2, PARTS, n_width, group)), dma((2, PARTS, n_width, group, n_grid)),
                dma((2, PARTS, n_width, group, ways)),
                dma((2, n_width)), dma((2, n_width)), dma((n_width,)), dma((n_width,)),
            ],
            compiler_params=pltpu.CompilerParams(
                collective_id=0, has_side_effects=True, vmem_limit_bytes=VMEM),
            cost_estimate=pl.CostEstimate(flops=flops, bytes_accessed=moved, transcendentals=0),
        )(query_acts, query_grads, act_inverse, grad_inverse, train_acts, train_grads)
        share = queries // n_width
        slots = lax.axis_index("width") * share + jnp.arange(share, dtype=jnp.int32)
        hit = query_slot[:, None] == slots[None, :]
        picked = jnp.sum(
            jnp.where(hit[:, :, None], table.reshape(queries, 1, tokens), 0.0), axis=0)
        return picked.T * resident[:, None].astype(f32)

    return jax.shard_map(
        local,
        mesh=mesh,
        in_specs=(
            P(("dp", "grid"), "width"),
            P(("dp", "grid"), "width"),
            P("dp", "width"),
            P("dp", "width"),
            P(("dp", "grid"), "width"),
            P(("dp", "grid"), "width"),
            P(),
            P(("dp", "grid")),
        ),
        out_specs=P(("dp", "grid"), "width"),
        check_vma=False,
    )
```
